32 devices in a mesh: prow: 4 (over x, core), pcol: 8 (over z, y).
Axes of the slice: x: 2, y: 2, z: 4, core: 2. Of those that a mesh axis runs over, the one named last changes fastest.
Arguments:
- front: float32 [8192, 8192], P('prow', 'pcol'), as said below
- parent_tile: int32 [32], replicated, may hold values from 0 to 31, as said below
Outputs:
- panel_factor: float32 [8192, 1024], P('prow')
- contribution: bfloat16 [8192, 8192], P('prow', 'pcol')
The draws below stay inside these ranges and needn't reach their ends.
Inputs may be any that keep to these rules, and one draw needn't show every extreme that they name: The front is symmetric positive definite in logical order, with smallest eigenvalue 0.5 or more. parent_tile is a permutation of the 32 tile indices. The tiles whose indices agree modulo 4 go to each such class of parent indices in groups of either none or exactly 2 tiles; tiles whose indices agree modulo 8 go to distinct classes of parent indices modulo 8.
All inputs are finite; a program needn't handle non-finite values.
Results may differ from the reference program's by a relative error of at most 0.001.
Values may be sent and summed in bfloat16 or wider, within the bound.
A program may use at most 192 MiB of HBM per device.

```python
import jax
import jax.numpy as jnp
from jax import lax

TS = 256
TC = 4
PANELS = 2
PW = 2
NT = 32
TR = 8
NF = 8192
N_PROW = 4
N_PCOL = 8


def draw_front(key, part):
    count = TC * N_PCOL
    order = count * TS
    rows_dev = count // N_PROW
    inner = 2 * PANELS * PW * TS
    first, second = jax.random.split(jax.random.fold_in(key, 11), 2)
    raw = jax.random.normal(first, (order, inner), jnp.float32)
    diag_vals = jax.random.uniform(second, (order,), jnp.float32, 0.5, 2.0)
    product = jnp.dot(raw, raw.T, precision=lax.Precision.HIGHEST) * (4.0 / inner)
    product = 0.5 * (product + product.T)
    index = jnp.arange(order)
    matrix = product.at[index, index].add(diag_vals)
    matrix = matrix.reshape(rows_dev, N_PROW, TS, order).transpose(1, 0, 2, 3).reshape(order, order)
    matrix = matrix.reshape(order, TC, N_PCOL, TS).transpose(0, 2, 1, 3).reshape(order, order)
    return matrix.astype(jnp.float32)


def draw_parent_tile(key, part):
    first, second, third = jax.random.split(jax.random.fold_in(key, 23), 3)
    fourth = jax.random.fold_in(key, 29)
    group = N_PCOL // N_PROW
    sigma = jax.random.permutation(first, N_PROW)
    shifts = jax.random.permutation(second, N_PROW)[:TC]
    blocks = jax.random.permutation(third, TC)
    offset = jax.random.randint(fourth, (), 0, group)
    flips = (jnp.arange(TC) + offset) % group
    index = jnp.arange(TC * N_PCOL)
    slot = index // N_PCOL
    rest = index % N_PCOL
    upper = (rest // N_PROW + flips[slot]) % group
    lower = rest % N_PROW
    result = N_PCOL * blocks[slot] + N_PROW * upper + (sigma[lower] + shifts[slot]) % N_PROW
    return result.astype(jnp.int32)


def setup_inputs(seed: int = 0) -> dict:
    splits = jax.random.split(jax.random.key(seed), 3)
    front = draw_front(jax.random.fold_in(splits[2], 71), 0)
    parent_tile = draw_parent_tile(jax.random.fold_in(splits[2], 71), 0)
    return {"front": front, "parent_tile": parent_tile}


def to_logical(stored):
    rows = stored.reshape(N_PROW, TR, TS, NF).transpose(1, 0, 2, 3).reshape(NF, NF)
    return rows.reshape(NF, N_PCOL, TC, TS).transpose(0, 2, 1, 3).reshape(NF, NF)

def rows_stored(matrix):
    width = matrix.shape[1]
    return matrix.reshape(TR, N_PROW, TS, width).transpose(1, 0, 2, 3).reshape(NF, width)

def cols_stored(matrix):
    return matrix.reshape(NF, TC, N_PCOL, TS).transpose(0, 2, 1, 3).reshape(NF, NF)

def reference(front, parent_tile):
    steps_total = PANELS * PW
    work = to_logical(front)
    columns = []
    for step in range(steps_total):
        low = step * TS
        high = low + TS
        factor = jnp.linalg.cholesky(work[low:high, low:high])
        below = work[high:, low:high]
        solved = jax.scipy.linalg.solve_triangular(factor, below.T, lower=True).T
        columns.append(jnp.concatenate([jnp.zeros((low, TS), jnp.float32), factor, solved], axis=0))
        update = jnp.dot(solved, solved.T, precision=lax.Precision.HIGHEST)
        work = work.at[high:, high:].add(-update)
    panel_factor = rows_stored(jnp.concatenate(columns, axis=1))
    index = jnp.arange(NF, dtype=jnp.int32)
    keep = (index >= steps_total * TS)[:, None] & (index >= steps_total * TS)[None, :]
    schur = jnp.where(keep, work, 0.0).astype(jnp.bfloat16)
    tiles = jnp.arange(NT, dtype=jnp.int32)
    inverse = jnp.sum(jnp.where(parent_tile[None, :] == tiles[:, None], tiles[None, :], 0), axis=1).astype(jnp.int32)
    blocks = schur.reshape(NT, TS, NT, TS)
    moved = jnp.take(jnp.take(blocks, inverse, axis=0), inverse, axis=2).reshape(NF, NF)
    contribution = cols_stored(rows_stored(moved))
    return (panel_factor, contribution)
```

```python
import jax
import jax.numpy as jnp
from jax import lax
from jax.experimental import pallas as pl
from jax.experimental.pallas import tpu as pltpu
from jax.sharding import PartitionSpec as P

TS = 256
PANELS = 2
PW = 2
BLOCK = 128
FULL = lax.Precision.HIGHEST


def eliminate(block):
    lane = lax.broadcasted_iota(jnp.int32, (BLOCK, BLOCK), 1)
    sub = lax.broadcasted_iota(jnp.int32, (BLOCK, BLOCK), 0)
    done = []
    rest = block
    for j in range(BLOCK):
        first = (j // 8) * 8
        here = j - first
        row = rest[here : here + 1, :]
        pivot = rest[here : here + 1, j : j + 1]
        scale = 1.0 / pivot
        at = lane[:1] == j
        pivot_row = jnp.where(at, 1.0, row) * scale
        factors = jnp.where(sub[first:] > j, rest[:, j : j + 1], 0.0)
        cleared = jnp.where((lane[first:] == j) & (sub[first:] > j), 0.0, rest)
        rest = cleared - factors * pivot_row
        if here == 7:
            done.append(rest[:8])
            rest = rest[8:]
    full = jnp.concatenate(done, axis=0)
    diagonal = jnp.sum(jnp.where(lane == sub, full, 0.0), axis=1, keepdims=True)
    root = lax.rsqrt(diagonal)
    upper = jnp.where(lane >= sub, full, 0.0) * root
    inverse = jnp.where(lane < sub, full, jnp.where(lane == sub, 1.0, 0.0)) * root
    return upper, inverse


def factor_kernel(front_ref, inverse_ref, work, panel):
    order = front_ref.shape[0]
    blocks = order // BLOCK
    work[...] = front_ref[...]
    inverse_ref[...] = jnp.where(
        lax.broadcasted_iota(jnp.int32, (order, order), 0)
        == lax.broadcasted_iota(jnp.int32, (order, order), 1),
        1.0,
        0.0,
    )

    @pl.loop(0, blocks)
    def _(k):
        start = pl.multiple_of(k * BLOCK, BLOCK)
        rows = pl.ds(start, BLOCK)
        _, inverse = eliminate(work[rows, rows])
        lanes = lax.broadcasted_iota(jnp.int32, (BLOCK, order), 1)
        top = jnp.dot(inverse, work[rows, :], precision=FULL, preferred_element_type=jnp.float32)
        panel[...] = jnp.where(lanes >= start + BLOCK, top, 0.0)
        inverse_ref[rows, :] = jnp.dot(
            inverse, inverse_ref[rows, :], precision=FULL, preferred_element_type=jnp.float32
        )

        @pl.loop(k + 1, blocks)
        def _(i):
            below = pl.ds(pl.multiple_of(i * BLOCK, BLOCK), BLOCK)
            left = panel[:, below].T
            work[below, :] -= jnp.dot(
                left, panel[...], precision=FULL, preferred_element_type=jnp.float32
            )
            inverse_ref[below, :] -= jnp.dot(
                left, inverse_ref[rows, :], precision=FULL, preferred_element_type=jnp.float32
            )


def inverse_factor(leading):
    order = leading.shape[0]
    return pl.pallas_call(
        factor_kernel,
        out_shape=jax.ShapeDtypeStruct((order, order), jnp.float32),
        in_specs=[pl.BlockSpec(memory_space=pltpu.VMEM)],
        out_specs=pl.BlockSpec(memory_space=pltpu.VMEM),
        scratch_shapes=[
            pltpu.VMEM((order, order), jnp.float32),
            pltpu.VMEM((BLOCK, order), jnp.float32),
        ],
        compiler_params=pltpu.CompilerParams(vmem_limit_bytes=32 * 1024 * 1024),
        cost_estimate=pl.CostEstimate(
            flops=20 * order**3, bytes_accessed=8 * order**2, transcendentals=0
        ),
    )(leading)


def panel_rows(front, prows, pcols, steps):
    tile_rows = front.shape[0] // TS
    tile_cols = front.shape[1] // TS
    group = pcols // prows
    col_id = lax.axis_index("pcol")
    pairs = [
        (k * pcols + g * prows + s, s * pcols + g * prows + k)
        for g in range(1, group)
        for k in range(prows)
        for s in range(prows)
    ]
    swapped = lax.ppermute(front[:TS], ("prow", "pcol"), pairs)
    swapped = swapped.T.reshape(tile_cols, TS, TS)
    native = front[:, :TS].reshape(tile_cols, group, TS, TS)[:, 0]
    mine = jnp.where(col_id < prows, native, swapped)
    every = lax.all_gather(mine, "pcol", axis=0, tiled=False)
    every = every.reshape(group, prows, tile_cols, TS, TS)[:, :steps]
    return every.transpose(2, 0, 3, 1, 4).reshape(tile_rows * TS, steps * TS)


def shards(front, parent_tile):
    prows = lax.axis_size("prow")
    pcols = lax.axis_size("pcol")
    row_id = lax.axis_index("prow")
    col_id = lax.axis_index("pcol")
    tile_rows = front.shape[0] // TS
    tile_cols = front.shape[1] // TS
    group = pcols // prows
    steps_total = PANELS * PW
    width = steps_total * TS
    assert steps_total <= prows and group * prows == pcols

    corner = lax.all_gather(front[:TS, :TS], "pcol", axis=0, tiled=False)[:steps_total]
    corner = corner.transpose(1, 0, 2).reshape(TS, width)
    strips = lax.all_gather(jnp.concatenate([corner, front[:TS]], axis=1), "prow", axis=0, tiled=True)
    strips = strips[:width]
    leading, front_cols = strips[:, :width], strips[:, width:]
    front_rows = panel_rows(front, prows, pcols, steps_total)

    inverse_low = inverse_factor(leading)
    factor_cols = jnp.dot(inverse_low, front_cols, precision=lax.Precision.HIGH)
    factor_rows = lax.dot_general(
        front_rows, inverse_low, (((1,), (1,)), ((), ())), precision=lax.Precision.HIGH
    )
    local = jnp.arange(tile_rows * TS, dtype=jnp.int32)
    row_pos = (local // TS * prows + row_id) * TS + local % TS
    panel_factor = jnp.where(
        row_pos[:, None] >= jnp.arange(width, dtype=jnp.int32)[None, :], factor_rows, 0.0
    )

    row_ids = jnp.arange(tile_rows, dtype=jnp.int32) * prows + row_id
    col_ids = jnp.arange(tile_cols, dtype=jnp.int32) * pcols + col_id
    keep = (row_ids >= steps_total)[:, None, None, None] & (col_ids >= steps_total)[
        None, None, :, None
    ]
    remaining = front - jnp.dot(panel_factor, factor_cols, precision=lax.Precision.HIGH)
    remaining = remaining.reshape(tile_rows, TS, tile_cols, TS)
    schur_part = jnp.where(keep, remaining, 0.0).astype(jnp.bfloat16)

    total = parent_tile.shape[0]
    every = jnp.arange(total, dtype=jnp.int32)
    inverse = jnp.sum(jnp.where(parent_tile[None, :] == every[:, None], every[None, :], 0), axis=1)
    row_dest = (parent_tile.reshape(tile_rows, prows) % prows).T
    earlier = jnp.arange(tile_rows)[:, None] > jnp.arange(tile_rows)[None, :]
    alike = row_dest[:, :, None] == row_dest[:, None, :]
    rank = jnp.sum(alike & earlier[None], axis=2)
    slot_of = row_dest * group + rank
    my_slots = lax.dynamic_index_in_dim(slot_of, row_id, 0, keepdims=False)
    row_slots = jnp.arange(prows * group, dtype=jnp.int32)
    send_rows = (row_slots[:, None] == my_slots[None, :]).astype(jnp.bfloat16)
    child_rows = inverse[jnp.arange(tile_rows, dtype=jnp.int32) * prows + row_id]
    source_row = child_rows % prows
    recv_index = source_row * group + rank[source_row, child_rows // prows]
    take_rows = (recv_index[:, None] == row_slots[None, :]).astype(jnp.bfloat16)
    col_dest = parent_tile[col_ids] % pcols
    col_slots = jnp.arange(pcols, dtype=jnp.int32)
    send_cols = (col_slots[:, None] == col_dest[None, :]).astype(jnp.bfloat16)
    child_cols = inverse[jnp.arange(tile_cols, dtype=jnp.int32) * pcols + col_id]
    take_cols = ((child_cols % pcols)[:, None] == col_slots[None, :]).astype(jnp.bfloat16)
    outgoing = jnp.einsum(
        "sl,lamb->samb", send_rows, schur_part, preferred_element_type=jnp.float32
    ).astype(jnp.bfloat16)
    arrived = lax.all_to_all(outgoing, "prow", split_axis=0, concat_axis=0, tiled=True)
    blocks = jnp.einsum(
        "ls,samb->lamb", take_rows, arrived, preferred_element_type=jnp.float32
    ).astype(jnp.bfloat16)
    outgoing = jnp.einsum(
        "em,lamb->elab", send_cols, blocks, preferred_element_type=jnp.float32
    ).astype(jnp.bfloat16)
    move_arrived = lax.all_to_all(outgoing, "pcol", split_axis=0, concat_axis=0, tiled=True)
    moved = jnp.einsum(
        "ns,slab->lanb", take_cols, move_arrived, preferred_element_type=jnp.float32
    ).astype(jnp.bfloat16)
    contribution = moved.reshape(tile_rows * TS, tile_cols * TS)
    return (panel_factor, contribution)


def solution(mesh):
    return jax.shard_map(
        shards,
        mesh=mesh,
        in_specs=(P("prow", "pcol"), P()),
        out_specs=(P("prow", None), P("prow", "pcol")),
        check_vma=False,
    )
```
